32 devices in a mesh: shots: 2 (over x), gx: 16 (over z, y, core).
Axes of the slice: x: 2, y: 2, z: 4, core: 2. Of those that a mesh axis runs over, the one named last changes fastest.
Arguments:
- displacement: float32 [3, 256, 256, 128], P(None, ('shots', 'gx')), parts along dimension 1, may hold values from -9 to 9
- adjoint: float32 [3, 256, 256, 128], P(None, ('shots', 'gx')), parts along dimension 1, may hold values from -6 to 6
- vp_model: float32 [256, 256, 128], P(('shots', 'gx')), parts along dimension 0, may hold values from 1.5 to 6
- vs_model: float32 [256, 256, 128], P(('shots', 'gx')), parts along dimension 0, may hold values from 0.8 to 3.5
Outputs:
- kernel_p: float32 [256, 256, 128], P(('shots', 'gx')), parts along dimension 0
- kernel_s: float32 [256, 256, 128], P(('shots', 'gx')), parts along dimension 0
The draws below stay inside these ranges and needn't reach their ends.
There are 2 independent parts, one for each index of `shots`. The reference program is written for one: setup_inputs(seed, part) draws one part's arguments, and reference() takes and returns one part's arrays. A program takes and returns all parts, laid end to end along the dimension named above; each array names one. Nothing has to cross between parts.
All inputs are finite; a program needn't handle non-finite values.
Results may differ from the reference program's by a relative error of at most 0.0001.
Values sent between devices are 32-bit elements; how exact they have to be, the bound alone decides.
A program may use at most 64 MiB of HBM per device.

```python
import math
import jax
import jax.numpy as jnp

NY = 256
NZ = 128
ITERS = 3
NX = 128


def smooth_profile(key, shift_range):
    keys = jax.random.split(key, 3)
    phases = jax.random.uniform(keys[0], (2,), minval=0.0, maxval=2.0 * math.pi)
    second_weight = jax.random.uniform(keys[1], (), minval=0.0, maxval=1.0)
    offset = jax.random.uniform(keys[2], (), minval=-shift_range, maxval=shift_range)
    position = jnp.arange(NX, dtype=jnp.float32) * (2.0 * math.pi / NX)
    profile = 0.5 + 0.35 * jnp.sin(position + phases[0]) + 0.25 * second_weight * jnp.sin(2.0 * position + phases[1]) + offset
    return jnp.clip(profile, 0.0, 1.0)[None, :, None, None]


def plane_waves(key, shortest, longest, modes):
    keys = jax.random.split(key, 5)
    polar_angle = jnp.arccos(jax.random.uniform(keys[0], (3, modes), minval=-1.0, maxval=1.0))
    azimuth = jax.random.uniform(keys[1], (3, modes), minval=0.0, maxval=2.0 * math.pi)
    wavelength = jnp.exp(jax.random.uniform(keys[2], (3, modes), minval=math.log(shortest), maxval=math.log(longest)))
    phase_shift = jax.random.uniform(keys[3], (3, modes), minval=0.0, maxval=2.0 * math.pi)
    amplitude = jax.random.uniform(keys[4], (3, modes), minval=0.5, maxval=1.0)
    wavenumber = 2.0 * math.pi / wavelength
    wave_x = wavenumber * jnp.sin(polar_angle) * jnp.cos(azimuth)
    wave_y = wavenumber * jnp.sin(polar_angle) * jnp.sin(azimuth)
    wave_z = wavenumber * jnp.cos(polar_angle)
    cells_x = jnp.arange(NX, dtype=jnp.float32)[None, :, None, None]
    cells_y = jnp.arange(NY, dtype=jnp.float32)[None, None, :, None]
    cells_z = jnp.arange(NZ, dtype=jnp.float32)[None, None, None, :]
    total = jnp.zeros((3, NX, NY, NZ), jnp.float32)
    for mode in range(modes):
        argument = wave_x[:, mode, None, None, None] * cells_x + wave_y[:, mode, None, None, None] * cells_y
        argument = argument + wave_z[:, mode, None, None, None] * cells_z + phase_shift[:, mode, None, None, None]
        total = total + amplitude[:, mode, None, None, None] * jnp.sin(argument)
    return total / modes


def draw_displacement(key, part):
    key = jax.random.fold_in(key, 11)
    keys = jax.random.split(key, 3)
    profile = smooth_profile(keys[0], 0.2)
    rough = jnp.clip(jax.random.normal(keys[1], (3, NX, NY, NZ), jnp.float32), -3.0, 3.0)
    smooth = plane_waves(keys[2], 6.0, 16.0, 3)
    weight_rough = 1.2 - 0.9 * profile
    weight_smooth = 0.3 + 2.7 * profile
    values = weight_rough * rough + weight_smooth * smooth
    return jnp.clip(values, -9.0, 9.0).astype(jnp.float32)


def steps_of(own_key, extent, pieces, low, high):
    gain, own = 1.0, jax.random.fold_in(own_key, 6)
    for axis_at, shards_of in pieces:
        draws = jnp.exp(jax.random.uniform(jax.random.fold_in(own, axis_at), (shards_of,), jnp.float32, low / len(pieces), high / len(pieces)))
        gain = gain * jnp.repeat(draws, extent[axis_at] // shards_of).reshape([-1 if axis == axis_at else 1 for axis in range(len(extent))])
    return gain


def scatter_about(key, extent, scale, limit, shards=(), kind=jnp.bfloat16):
    factor_of = steps_of(key, extent, shards, -0.22, 0.18) if shards else 1.0
    result = jax.random.normal(key, extent, jnp.float32) * scale * factor_of
    return jnp.minimum(jnp.maximum(result, -limit), limit).astype(kind)


def setup_inputs(seed: int = 0, part: int = 0) -> dict:
    key_list = jax.random.split(jax.random.key(seed), 5)
    part_keys = jax.random.split(jax.random.fold_in(key_list[4], part), 5)
    displacement = draw_displacement(jax.random.fold_in(jax.random.fold_in(key_list[4], part), 71), part)
    adjoint = scatter_about(part_keys[1], (3, NX, NY, NZ), 1.0, 6.0, ((1, 16),), jnp.float32)
    vp_model = jnp.clip(jnp.exp(math.log(6.0) - 1.3862944 * jax.random.uniform(part_keys[2], (NX, NY, NZ), jnp.float32) ** steps_of(part_keys[2], (NX, NY, NZ), ((0, 16),), -0.2, 0.2)), 1.5, 6.0)
    vs_model = jnp.clip(jnp.exp(math.log(3.5) - 1.4759065 * jax.random.uniform(part_keys[3], (NX, NY, NZ), jnp.float32) ** steps_of(part_keys[3], (NX, NY, NZ), ((0, 16),), -0.2, 0.2)), 0.8, 3.5)
    return {"displacement": displacement, "adjoint": adjoint, "vp_model": vp_model, "vs_model": vs_model}


def derive(field):
    padded = jnp.pad(field, ((0, 0), (1, 1), (1, 1), (1, 1)))
    along_x = (padded[:, 2:, 1:-1, 1:-1] - padded[:, :-2, 1:-1, 1:-1]) / 2.0
    along_y = (padded[:, 1:-1, 2:, 1:-1] - padded[:, 1:-1, :-2, 1:-1]) / 2.0
    along_z = (padded[:, 1:-1, 1:-1, 2:] - padded[:, 1:-1, 1:-1, :-2]) / 2.0
    return along_x, along_y, along_z


def operate(field):
    padded = jnp.pad(field, ((0, 0), (1, 1), (1, 1), (1, 1)))
    beside = padded[:, 2:, 1:-1, 1:-1] + padded[:, :-2, 1:-1, 1:-1]
    beside = beside + padded[:, 1:-1, 2:, 1:-1] + padded[:, 1:-1, :-2, 1:-1]
    beside = beside + padded[:, 1:-1, 1:-1, 2:] + padded[:, 1:-1, 1:-1, :-2]
    return 6.0 * field - beside


def totals(values):
    return jnp.sum(values, axis=(1, 2, 3))


def expand(values):
    return values[:, None, None, None]


def reference(displacement, adjoint, vp_model, vs_model):
    along_x, along_y, along_z = derive(displacement)
    divergence = along_x[0] + along_y[1] + along_z[2]
    rhs = jnp.stack([-divergence, along_y[2] - along_z[1], along_z[0] - along_x[2], along_x[1] - along_y[0]])
    solution = jnp.zeros_like(rhs)
    residual = rhs
    direction = rhs
    norm_now = totals(residual * residual)
    for iteration in range(ITERS):
        image = operate(direction)
        alpha = norm_now / totals(direction * image)
        solution = solution + expand(alpha) * direction
        residual = residual - expand(alpha) * image
        norm_next = totals(residual * residual)
        direction = residual + expand(norm_next / norm_now) * direction
        norm_now = norm_next
    along_x, along_y, along_z = derive(solution)
    p_sum = along_x[0] * adjoint[0] + along_y[0] * adjoint[1] + along_z[0] * adjoint[2]
    s_sum = (along_y[3] - along_z[2]) * adjoint[0] + (along_z[1] - along_x[3]) * adjoint[1] + (along_x[2] - along_y[1]) * adjoint[2]
    return vp_model * p_sum, vs_model * s_sum
```

```python
import functools

import jax
import jax.numpy as jnp
from jax import lax
from jax.experimental import pallas as pl
from jax.experimental.pallas import tpu as pltpu
from jax.sharding import PartitionSpec as P

ITERS = 3
DEPTH = 4
PAD = 8
CHUNK = 32
F32 = jnp.float32
MESH = pl.DeviceIdType.MESH


def kernel(n, nx, ny, nz, u_hbm, adj_hbm, vp_hbm, vs_hbm, kp_hbm, ks_hbm,
           u, basis0, basis1, basis2, parts, adj, vp, vs, out, acc, mom, local_sem,
           send_sem, recv_sem, mom_send, mom_recv, out_sem):
    me = lax.axis_index("gx")
    right, left = lax.rem(me + 1, n), lax.rem(me + n - 1, n)
    has_left, has_right = me > 0, me < n - 1
    bases = (basis0, basis1, basis2)

    loads = [
        pltpu.make_async_copy(u_hbm, u.at[:, pl.ds(DEPTH, nx), pl.ds(PAD, ny)], local_sem.at[0]),
        pltpu.make_async_copy(adj_hbm, adj, local_sem.at[1]),
        pltpu.make_async_copy(vp_hbm, vp, local_sem.at[2]),
        pltpu.make_async_copy(vs_hbm, vs, local_sem.at[3]),
    ]
    loads[0].start()

    barrier = pltpu.get_barrier_semaphore()

    def greet(t, carry):
        pl.semaphore_signal(barrier, inc=1, device_id={"gx": lax.rem(me + t, n)}, device_id_type=MESH)
        return carry

    lax.fori_loop(1, n, greet, 0)
    loads[1].start()

    for ref in (u,) + bases:
        zero = jnp.zeros(ref.shape[:2] + (PAD, nz), F32)
        ref[:, :, pl.ds(0, PAD), :] = zero
        ref[:, :, pl.ds(PAD + ny, PAD), :] = zero
    acc[...] = jnp.zeros_like(acc)

    @pl.when(jnp.logical_not(has_left))
    def _():
        u[:, pl.ds(0, DEPTH)] = jnp.zeros((3, DEPTH) + u.shape[2:], F32)

    @pl.when(jnp.logical_not(has_right))
    def _():
        u[:, pl.ds(DEPTH + nx, DEPTH)] = jnp.zeros((3, DEPTH) + u.shape[2:], F32)

    pl.semaphore_wait(barrier, n - 1)

    rights, lefts = [], []
    for d in range(1, DEPTH + 1):
        rights.append(pltpu.make_async_remote_copy(
            src_ref=u_hbm.at[:, nx - d], dst_ref=u.at[:, DEPTH - d, pl.ds(PAD, ny)],
            send_sem=send_sem.at[0, d - 1], recv_sem=recv_sem.at[0, d - 1],
            device_id={"gx": right}, device_id_type=MESH))
        lefts.append(pltpu.make_async_remote_copy(
            src_ref=u_hbm.at[:, d - 1], dst_ref=u.at[:, DEPTH + nx + d - 1, pl.ds(PAD, ny)],
            send_sem=send_sem.at[1, d - 1], recv_sem=recv_sem.at[1, d - 1],
            device_id={"gx": left}, device_id_type=MESH))

        @pl.when(has_right)
        def _():
            rights[-1].start()

        @pl.when(has_left)
        def _():
            lefts[-1].start()
    loads[2].start()
    loads[3].start()

    lane = lax.broadcasted_iota(jnp.int32, (CHUNK, nz), 1)
    first, last = lane == 0, lane == nz - 1
    inside_left = jnp.where(has_left, 1.0, 0.0).astype(F32)
    inside_right = jnp.where(has_right, 1.0, 0.0).astype(F32)

    def before(value):
        return jnp.where(first, 0.0, pltpu.roll(value, 1, 1))

    def after(value):
        return jnp.where(last, 0.0, pltpu.roll(value, nz - 1, 1))

    def fold(value):
        return jnp.sum(value.reshape(CHUNK // 8, 8, nz), axis=0)

    def shifted(ref, k, p, row, step):
        return ref[k, p, pl.ds(row + step, CHUNK), :]

    def rhs(plane, row, scale):
        def d_x(k):
            return u[k, plane + 1, pl.ds(row, CHUNK), :] - u[k, plane - 1, pl.ds(row, CHUNK), :]

        def d_y(k):
            return shifted(u, k, plane, row, 1) - shifted(u, k, plane, row, -1)

        def d_z(k):
            value = u[k, plane, pl.ds(row, CHUNK), :]
            return after(value) - before(value)

        half = 0.5 if scale is None else 0.5 * scale
        values = (-(d_x(0) + d_y(1) + d_z(2)), d_y(2) - d_z(1), d_z(0) - d_x(2), d_x(1) - d_y(0))
        for k, value in enumerate(values):
            basis0[k, plane - 1, pl.ds(row, CHUNK), :] = value * half

    def stage(j, plane, row, scale, owned):
        source, p = bases[j], plane - 1 - j
        if owned:
            a = [adj[c, plane - DEPTH, pl.ds(row - PAD, CHUNK), :] for c in range(3)]
        sums = []
        for k in range(4):
            mid = source[k, p, pl.ds(row, CHUNK), :]
            xm, xp = source[k, p - 1, pl.ds(row, CHUNK), :], source[k, p + 1, pl.ds(row, CHUNK), :]
            ym, yp = shifted(source, k, p, row, -1), shifted(source, k, p, row, 1)
            zm, zp = before(mid), after(mid)
            image = 6.0 * mid - ((xm + xp) + (ym + yp) + (zm + zp))
            if j < 2:
                bases[j + 1][k, plane - 2 - j, pl.ds(row, CHUNK), :] = image if scale is None else image * scale
            if owned:
                sums.append(fold(mid * mid))
                sums.append(fold(mid * image))
                if k == 0:
                    part = (xp - xm) * a[0] + (yp - ym) * a[1] + (zp - zm) * a[2]
                elif k == 1:
                    part = (zp - zm) * a[1] - (yp - ym) * a[2]
                elif k == 2:
                    part = (xp - xm) * a[2] - (zp - zm) * a[0]
                else:
                    part = (yp - ym) * a[0] - (xp - xm) * a[1]
                parts[j, k, plane - DEPTH, pl.ds(row - PAD, CHUNK), :] = part
        return tuple(sums)

    chunks = ny // CHUNK

    def row_of(c):
        return pl.multiple_of(PAD + c * CHUNK, 8)

    def run_rhs(low, high, scale=None):
        def step(i, carry):
            rhs(low + i // chunks, row_of(i % chunks), scale)
            return carry
        lax.fori_loop(0, (high - low + 1) * chunks, step, 0)

    def run_stage(j, low, high, owned, scale=None):
        zero = jnp.zeros((8, nz), F32)
        def step(i, carry):
            sums = stage(j, low + i // chunks, row_of(i % chunks), scale, owned)
            return tuple(x + y for x, y in zip(carry, sums))
        sums = lax.fori_loop(0, (high - low + 1) * chunks, step, (zero,) * (8 if owned else 0))
        if owned:
            for k in range(4):
                acc[2 * j, k] += sums[2 * k]
                acc[2 * j + 1, k] += sums[2 * k + 1]

    lo, hi = DEPTH, DEPTH + nx - 1
    loads[0].wait()
    run_rhs(lo + 1, hi - 1)
    loads[1].wait()
    run_stage(0, lo + 2, hi - 2, True)
    run_stage(1, lo + 3, hi - 3, True)

    for d in range(1, DEPTH + 1):
        for side in range(2):
            inside = inside_left if side == 0 else inside_right

            @pl.when(has_left if side == 0 else has_right)
            def _():
                (rights if side == 0 else lefts)[d - 1].wait_recv()

            def at(offset):
                return lo + offset - d if side == 0 else hi - offset + d

            run_rhs(at(1), at(1), inside if d > 1 else None)
            for j in range(3):
                plane = at(2 + j)
                owned = d <= 2 + j
                run_stage(j, plane, plane, owned, None if owned else inside)

    rows = lax.broadcasted_iota(jnp.int32, (8, nz), 0)
    lanes = lax.broadcasted_iota(jnp.int32, (8, nz), 1)
    message = jnp.zeros((8, nz), F32)
    for m in range(6):
        tile = jnp.zeros((8, nz), F32)
        for k in range(4):
            tile = jnp.where(rows == k, jnp.sum(acc[m, k], axis=0, keepdims=True), tile)
        message = jnp.where(lanes == m, jnp.sum(tile, axis=1, keepdims=True), message)
    mom[me] = message

    def tell(t, carry):
        there = lax.rem(me + t, n)
        pltpu.make_async_remote_copy(
            src_ref=mom.at[me], dst_ref=mom.at[me], send_sem=mom_send.at[t],
            recv_sem=mom_recv.at[me], device_id={"gx": there}, device_id_type=MESH).start()
        return carry

    def hear(t, carry):
        source = lax.rem(me + t, n)
        pltpu.make_async_remote_copy(
            src_ref=mom.at[me], dst_ref=mom.at[source], send_sem=mom_send.at[t],
            recv_sem=mom_recv.at[source], device_id={"gx": source}, device_id_type=MESH).wait_recv()
        return carry

    lax.fori_loop(1, n, tell, 0)
    lax.fori_loop(1, n, hear, 0)
    total = lax.fori_loop(0, n, lambda t, carry: carry + mom[t], jnp.zeros((8, nz), F32))
    mu = [jnp.broadcast_to(jnp.sum(jnp.where(lanes == m, total, 0.0), axis=1, keepdims=True), (8, nz))
          for m in range(6)]

    def quad(c, shift):
        value = None
        for i in range(len(c)):
            for j in range(i, len(c)):
                term = (c[i] * c[j]) * mu[i + j + shift]
                if i != j:
                    term = term + term
                value = term if value is None else value + term
        return value

    one = jnp.ones((8, nz), F32)
    residual, direction, norm = [one], [one], mu[0]
    coefs = [jnp.zeros((8, nz), F32)] * ITERS
    for iteration in range(ITERS):
        alpha = norm / quad(direction, 1)
        for i, value in enumerate(direction):
            coefs[i] = coefs[i] + alpha * value
        if iteration + 1 < ITERS:
            image = [None] + [alpha * value for value in direction]
            residual = residual + [jnp.zeros((8, nz), F32)]
            residual = [r if v is None else r - v for r, v in zip(residual, image)]
            new = quad(residual, 0)
            beta = new / norm
            direction = [r + beta * v for r, v in zip(residual, direction + [jnp.zeros((8, nz), F32)])]
            norm = new
    weight = [[jnp.broadcast_to(0.5 * coefs[j][k:k + 1, :], (CHUNK, nz)) for k in range(4)] for j in range(3)]

    loads[2].wait()
    loads[3].wait()

    def finish(plane):
        def step(c, carry):
            rows_at = pl.ds(pl.multiple_of(c * CHUNK, 8), CHUNK)
            p_sum = weight[0][0] * parts[0, 0, plane, rows_at, :]
            for j in range(1, 3):
                p_sum = p_sum + weight[j][0] * parts[j, 0, plane, rows_at, :]
            s_sum = None
            for k in range(1, 4):
                for j in range(3):
                    term = weight[j][k] * parts[j, k, plane, rows_at, :]
                    s_sum = term if s_sum is None else s_sum + term
            out[0, plane, rows_at, :] = vp[plane, rows_at, :] * p_sum
            out[1, plane, rows_at, :] = vs[plane, rows_at, :] * s_sum
            return carry
        lax.fori_loop(0, chunks, step, 0)

    stores = []
    for plane in range(nx):
        finish(plane)
        for o, target in enumerate((kp_hbm, ks_hbm)):
            stores.append(pltpu.make_async_copy(out.at[o, plane], target.at[plane], out_sem.at[o, plane]))
            stores[-1].start()

    def sent(t, carry):
        pltpu.make_async_remote_copy(
            src_ref=mom.at[me], dst_ref=mom.at[me], send_sem=mom_send.at[t],
            recv_sem=mom_recv.at[me], device_id={"gx": lax.rem(me + t, n)}, device_id_type=MESH).wait_send()
        return carry

    lax.fori_loop(1, n, sent, 0)
    for d in range(DEPTH):
        @pl.when(has_right)
        def _():
            rights[d].wait_send()

        @pl.when(has_left)
        def _():
            lefts[d].wait_send()
    for store in stores:
        store.wait()


def per_device(displacement, adjoint, vp_model, vs_model):
    n = lax.axis_size("gx")
    _, nx, ny, nz = displacement.shape
    tall = ny + 2 * PAD
    any_space = pl.BlockSpec(memory_space=pl.ANY)
    shape = jax.ShapeDtypeStruct((nx, ny, nz), F32)
    return pl.pallas_call(
        functools.partial(kernel, n, nx, ny, nz),
        out_shape=(shape, shape),
        in_specs=[any_space] * 4,
        out_specs=(any_space, any_space),
        scratch_shapes=[
            pltpu.VMEM((3, nx + 8, tall, nz), F32),
            pltpu.VMEM((4, nx + 6, tall, nz), F32),
            pltpu.VMEM((4, nx + 4, tall, nz), F32),
            pltpu.VMEM((4, nx + 2, tall, nz), F32),
            pltpu.VMEM((3, 4, nx, ny, nz), F32),
            pltpu.VMEM((3, nx, ny, nz), F32),
            pltpu.VMEM((nx, ny, nz), F32),
            pltpu.VMEM((nx, ny, nz), F32),
            pltpu.VMEM((2, nx, ny, nz), F32),
            pltpu.VMEM((6, 4, 8, nz), F32),
            pltpu.VMEM((n, 8, nz), F32),
            pltpu.SemaphoreType.DMA((4,)),
            pltpu.SemaphoreType.DMA((2, DEPTH)),
            pltpu.SemaphoreType.DMA((2, DEPTH)),
            pltpu.SemaphoreType.DMA((n,)),
            pltpu.SemaphoreType.DMA((n,)),
            pltpu.SemaphoreType.DMA((2, nx)),
        ],
        compiler_params=pltpu.CompilerParams(
            collective_id=0, has_side_effects=True, vmem_limit_bytes=56 * 1024 * 1024
        ),
    )(displacement, adjoint, vp_model, vs_model)


def solution(mesh):
    in_specs = (
        P(None, ("shots", "gx"), None, None),
        P(None, ("shots", "gx"), None, None),
        P(("shots", "gx"), None, None),
        P(("shots", "gx"), None, None),
    )
    out_specs = (P(("shots", "gx"), None, None), P(("shots", "gx"), None, None))
    return jax.shard_map(
        per_device, mesh=mesh, in_specs=in_specs, out_specs=out_specs, check_vma=False
    )
```

```python
import functools

import jax
import jax.numpy as jnp
from jax import lax
from jax.experimental import pallas as pl
from jax.experimental.pallas import tpu as pltpu
from jax.sharding import PartitionSpec as P

ITERS = 3
DEPTH = 4
PAD = 8
CHUNK = 256
WRITE = 64
SHIFT = 4.0
F32 = jnp.float32
MESH = pl.DeviceIdType.MESH


def kernel(n, nx, ny, nz, u_hbm, adj_hbm, p_out, s_out,
           u, basis0, basis1, basis2, parts, adj, acc, mom, local_sem,
           send_sem, recv_sem, mom_send, mom_recv):
    me = lax.axis_index("gx")
    right, left = lax.rem(me + 1, n), lax.rem(me + n - 1, n)
    has_left, has_right = me > 0, me < n - 1
    bases = (basis0, basis1, basis2)

    loads = [
        pltpu.make_async_copy(u_hbm, u.at[:, pl.ds(DEPTH, nx), pl.ds(PAD, ny)], local_sem.at[0]),
        pltpu.make_async_copy(adj_hbm, adj, local_sem.at[1]),
    ]
    loads[0].start()

    barrier = pltpu.get_barrier_semaphore()

    def greet(t, carry):
        pl.semaphore_signal(barrier, inc=1, device_id={"gx": lax.rem(me + t, n)}, device_id_type=MESH)
        return carry

    lax.fori_loop(1, n, greet, 0)
    loads[1].start()

    for ref in (u,) + bases:
        zero = jnp.zeros(ref.shape[:2] + (PAD, nz), F32)
        ref[:, :, pl.ds(0, PAD), :] = zero
        ref[:, :, pl.ds(PAD + ny, PAD), :] = zero
    acc[...] = jnp.zeros_like(acc)

    @pl.when(jnp.logical_not(has_left))
    def _():
        u[:, pl.ds(0, DEPTH)] = jnp.zeros((3, DEPTH) + u.shape[2:], F32)

    @pl.when(jnp.logical_not(has_right))
    def _():
        u[:, pl.ds(DEPTH + nx, DEPTH)] = jnp.zeros((3, DEPTH) + u.shape[2:], F32)

    pl.semaphore_wait(barrier, n - 1)

    rights, lefts = [], []
    for d in range(1, DEPTH + 1):
        rights.append(pltpu.make_async_remote_copy(
            src_ref=u_hbm.at[:, nx - d], dst_ref=u.at[:, DEPTH - d, pl.ds(PAD, ny)],
            send_sem=send_sem.at[0, d - 1], recv_sem=recv_sem.at[0, d - 1],
            device_id={"gx": right}, device_id_type=MESH))
        lefts.append(pltpu.make_async_remote_copy(
            src_ref=u_hbm.at[:, d - 1], dst_ref=u.at[:, DEPTH + nx + d - 1, pl.ds(PAD, ny)],
            send_sem=send_sem.at[1, d - 1], recv_sem=recv_sem.at[1, d - 1],
            device_id={"gx": left}, device_id_type=MESH))

        @pl.when(has_right)
        def _():
            rights[-1].start()

        @pl.when(has_left)
        def _():
            lefts[-1].start()

    lane = lax.broadcasted_iota(jnp.int32, (CHUNK, nz), 1)
    first, last = lane == 0, lane == nz - 1
    inside_left = jnp.where(has_left, 1.0, 0.0).astype(F32)
    inside_right = jnp.where(has_right, 1.0, 0.0).astype(F32)

    def before(value):
        return jnp.where(first, 0.0, pltpu.roll(value, 1, 1))

    def after(value):
        return jnp.where(last, 0.0, pltpu.roll(value, nz - 1, 1))

    def fold(value):
        return jnp.sum(value.reshape(CHUNK // 8, 8, nz), axis=0)

    def shifted(ref, k, p, row, step):
        return ref[k, p, pl.ds(row + step, CHUNK), :]

    def rhs(plane, row, scale):
        def d_x(k):
            return u[k, plane + 1, pl.ds(row, CHUNK), :] - u[k, plane - 1, pl.ds(row, CHUNK), :]

        def d_y(k):
            return shifted(u, k, plane, row, 1) - shifted(u, k, plane, row, -1)

        def d_z(k):
            value = u[k, plane, pl.ds(row, CHUNK), :]
            return after(value) - before(value)

        half = 0.5 if scale is None else 0.5 * scale
        values = (-(d_x(0) + d_y(1) + d_z(2)), d_y(2) - d_z(1), d_z(0) - d_x(2), d_x(1) - d_y(0))
        for k, value in enumerate(values):
            basis0[k, plane - 1, pl.ds(row, CHUNK), :] = value * half

    def stage(j, plane, row, scale, owned):
        source, p = bases[j], plane - 1 - j
        if owned:
            a = [adj[c, plane - DEPTH, pl.ds(row - PAD, CHUNK), :] for c in range(3)]
        sums = []
        for k in range(4):
            mid = source[k, p, pl.ds(row, CHUNK), :]
            xm, xp = source[k, p - 1, pl.ds(row, CHUNK), :], source[k, p + 1, pl.ds(row, CHUNK), :]
            ym, yp = shifted(source, k, p, row, -1), shifted(source, k, p, row, 1)
            zm, zp = before(mid), after(mid)
            image = (6.0 - SHIFT) * mid - ((xm + xp) + (ym + yp) + (zm + zp))
            if j < 2:
                bases[j + 1][k, plane - 2 - j, pl.ds(row, CHUNK), :] = image if scale is None else image * scale
            if owned:
                sums.append(fold(mid * mid))
                sums.append(fold(mid * image))
                if k == 0:
                    part = (xp - xm) * a[0] + (yp - ym) * a[1] + (zp - zm) * a[2]
                elif k == 1:
                    part = (zp - zm) * a[1] - (yp - ym) * a[2]
                elif k == 2:
                    part = (xp - xm) * a[2] - (zp - zm) * a[0]
                else:
                    part = (yp - ym) * a[0] - (xp - xm) * a[1]
                parts[j, k, plane - DEPTH, pl.ds(row - PAD, CHUNK), :] = part
        return tuple(sums)

    chunks = ny // CHUNK

    def row_of(c):
        return pl.multiple_of(PAD + c * CHUNK, 8)

    def run_rhs(low, high, scale=None):
        def step(i, carry):
            rhs(low + i // chunks, row_of(i % chunks), scale)
            return carry
        lax.fori_loop(0, (high - low + 1) * chunks, step, 0)

    def run_stage(j, low, high, owned, scale=None):
        zero = jnp.zeros((8, nz), F32)
        def step(i, carry):
            sums = stage(j, low + i // chunks, row_of(i % chunks), scale, owned)
            return tuple(x + y for x, y in zip(carry, sums))
        sums = lax.fori_loop(0, (high - low + 1) * chunks, step, (zero,) * (8 if owned else 0))
        if owned:
            for k in range(4):
                acc[2 * j, k] += sums[2 * k]
                acc[2 * j + 1, k] += sums[2 * k + 1]

    lo, hi = DEPTH, DEPTH + nx - 1
    loads[0].wait()
    run_rhs(lo + 1, hi - 1)
    loads[1].wait()
    run_stage(0, lo + 2, hi - 2, True)
    run_stage(1, lo + 3, hi - 3, True)

    for d in range(1, DEPTH + 1):
        for side in range(2):
            inside = inside_left if side == 0 else inside_right

            @pl.when(has_left if side == 0 else has_right)
            def _():
                (rights if side == 0 else lefts)[d - 1].wait_recv()

            def at(offset):
                return lo + offset - d if side == 0 else hi - offset + d

            run_rhs(at(1), at(1), inside if d > 1 else None)
            for j in range(3):
                plane = at(2 + j)
                owned = d <= 2 + j
                run_stage(j, plane, plane, owned, None if owned else inside)

    rows = lax.broadcasted_iota(jnp.int32, (8, nz), 0)
    lanes = lax.broadcasted_iota(jnp.int32, (8, nz), 1)
    message = jnp.zeros((8, nz), F32)
    for m in range(6):
        tile = jnp.zeros((8, nz), F32)
        for k in range(4):
            tile = jnp.where(rows == k, jnp.sum(acc[m, k], axis=0, keepdims=True), tile)
        message = jnp.where(lanes == m, jnp.sum(tile, axis=1, keepdims=True), message)
    mom[me] = message

    def tell(t, carry):
        there = lax.rem(me + t, n)
        pltpu.make_async_remote_copy(
            src_ref=mom.at[me], dst_ref=mom.at[me], send_sem=mom_send.at[t],
            recv_sem=mom_recv.at[me], device_id={"gx": there}, device_id_type=MESH).start()
        return carry

    def hear(t, carry):
        source = lax.rem(me + t, n)
        pltpu.make_async_remote_copy(
            src_ref=mom.at[me], dst_ref=mom.at[source], send_sem=mom_send.at[t],
            recv_sem=mom_recv.at[source], device_id={"gx": source}, device_id_type=MESH).wait_recv()
        return carry

    lax.fori_loop(1, n, tell, 0)
    lax.fori_loop(1, n, hear, 0)
    total = lax.fori_loop(0, n, lambda t, carry: carry + mom[t], jnp.zeros((8, nz), F32))
    mu = [jnp.broadcast_to(jnp.sum(jnp.where(lanes == m, total, 0.0), axis=1, keepdims=True), (8, nz))
          for m in range(6)]

    energy = [SHIFT * mu[m] + mu[m + 1] for m in range(5)]

    def quad(c, sums):
        value = None
        for i in range(len(c)):
            for j in range(i, len(c)):
                term = (c[i] * c[j]) * sums[i + j]
                if i != j:
                    term = term + term
                value = term if value is None else value + term
        return value

    one = jnp.ones((8, nz), F32)
    residual, direction, norm = [one], [one], mu[0]
    coefs = [jnp.zeros((8, nz), F32)] * ITERS
    for iteration in range(ITERS):
        alpha = norm / quad(direction, energy)
        for i, value in enumerate(direction):
            coefs[i] = coefs[i] + alpha * value
        if iteration + 1 < ITERS:
            none = [jnp.zeros((8, nz), F32)]
            image = [SHIFT * v + w for v, w in zip(direction + none, none + direction)]
            residual = [r - alpha * v for r, v in zip(residual + none, image)]
            new = quad(residual, mu)
            beta = new / norm
            direction = [r + beta * v for r, v in zip(residual, direction + none)]
            norm = new
    weight = [[jnp.broadcast_to(0.5 * coefs[j][k:k + 1, :], (WRITE, nz)) for k in range(4)] for j in range(3)]

    def finish(plane):
        def step(c, carry):
            rows_at = pl.ds(pl.multiple_of(c * WRITE, 8), WRITE)
            p_sum = weight[0][0] * parts[0, 0, plane, rows_at, :]
            for j in range(1, 3):
                p_sum = p_sum + weight[j][0] * parts[j, 0, plane, rows_at, :]
            s_sum = None
            for k in range(1, 4):
                for j in range(3):
                    term = weight[j][k] * parts[j, k, plane, rows_at, :]
                    s_sum = term if s_sum is None else s_sum + term
            p_out[plane, rows_at, :] = p_sum
            s_out[plane, rows_at, :] = s_sum
            return carry
        lax.fori_loop(0, ny // WRITE, step, 0)

    lax.fori_loop(0, nx, lambda plane, carry: (finish(plane), carry)[1], 0)

    def sent(t, carry):
        pltpu.make_async_remote_copy(
            src_ref=mom.at[me], dst_ref=mom.at[me], send_sem=mom_send.at[t],
            recv_sem=mom_recv.at[me], device_id={"gx": lax.rem(me + t, n)}, device_id_type=MESH).wait_send()
        return carry

    lax.fori_loop(1, n, sent, 0)
    for d in range(DEPTH):
        @pl.when(has_right)
        def _():
            rights[d].wait_send()

        @pl.when(has_left)
        def _():
            lefts[d].wait_send()


def per_device(displacement, adjoint, vp_model, vs_model):
    n = lax.axis_size("gx")
    _, nx, ny, nz = displacement.shape
    tall = ny + 2 * PAD
    any_space = pl.BlockSpec(memory_space=pl.ANY)
    shape = jax.ShapeDtypeStruct((nx, ny, nz), F32)
    p_sum, s_sum = pl.pallas_call(
        functools.partial(kernel, n, nx, ny, nz),
        out_shape=(shape, shape),
        in_specs=[any_space] * 2,
        out_specs=(pl.BlockSpec(memory_space=pltpu.VMEM),) * 2,
        scratch_shapes=[
            pltpu.VMEM((3, nx + 8, tall, nz), F32),
            pltpu.VMEM((4, nx + 6, tall, nz), F32),
            pltpu.VMEM((4, nx + 4, tall, nz), F32),
            pltpu.VMEM((4, nx + 2, tall, nz), F32),
            pltpu.VMEM((3, 4, nx, ny, nz), F32),
            pltpu.VMEM((3, nx, ny, nz), F32),
            pltpu.VMEM((6, 4, 8, nz), F32),
            pltpu.VMEM((n, 8, nz), F32),
            pltpu.SemaphoreType.DMA((2,)),
            pltpu.SemaphoreType.DMA((2, DEPTH)),
            pltpu.SemaphoreType.DMA((2, DEPTH)),
            pltpu.SemaphoreType.DMA((n,)),
            pltpu.SemaphoreType.DMA((n,)),
        ],
        compiler_params=pltpu.CompilerParams(
            collective_id=0, has_side_effects=True, vmem_limit_bytes=56 * 1024 * 1024
        ),
    )(displacement, adjoint)
    return vp_model * p_sum, vs_model * s_sum


def solution(mesh):
    in_specs = (
        P(None, ("shots", "gx"), None, None),
        P(None, ("shots", "gx"), None, None),
        P(("shots", "gx"), None, None),
        P(("shots", "gx"), None, None),
    )
    out_specs = (P(("shots", "gx"), None, None), P(("shots", "gx"), None, None))
    return jax.shard_map(
        per_device, mesh=mesh, in_specs=in_specs, out_specs=out_specs, check_vma=False
    )
```
